32 devices in a mesh: polar: 8 (over z, core), azimuth: 4 (over y, x).
Axes of the slice: x: 2, y: 2, z: 4, core: 2. Of those that a mesh axis runs over, the one named last changes fastest.
Arguments:
- signal: bfloat16 [512, 768, 256], P('polar', 'azimuth'), may hold values from -6 to 6
- cotangent: bfloat16 [512, 768, 256], P('polar', 'azimuth'), may hold values from -6 to 6
- mixing: bfloat16 [2, 256, 256], replicated, may hold values from -0.25 to 0.25
- coupling: bfloat16 [8, 6, 64, 64], replicated, may hold values from -0.75 to 0.75
- filters: float32 [8, 6, 2, 384], P(None, None, None, 'azimuth'), may hold values from -4 to 4
- band_counts: int32 [8], replicated, may hold values from 2 to 6, as said below
- band_offsets: int32 [8, 6], replicated, may hold values from -1 to 1, as said below
- band_basis: int32 [8, 6], replicated, may hold values from 0 to 1
Outputs:
- output: bfloat16 [512, 768, 256], P('polar', 'azimuth')
- signal_grad: bfloat16 [512, 768, 256], P('polar', 'azimuth')
The draws below stay inside these ranges and needn't reach their ends.
Inputs may be any that keep to these rules, and one draw needn't show every extreme that they name: `band_counts`: blocks 1 and 6 use all 6 slots; the two end blocks use at most 4. `band_offsets`: for every block b, the first band_counts[b] slots name distinct pairs of offset and basis, and b plus the offset lies in 0 to 7; later slots are unused.
All inputs are finite; a program needn't handle non-finite values.
Results may differ from the reference program's by a relative error of at most 0.0075.
Values may be sent and summed in bfloat16 or wider, within the bound.
A program may use at most 192 MiB of HBM per device.

```python
import math
import jax
import jax.numpy as jnp
from jax import lax

C = 256
NLON = 768
M = 384
K = 2
BLOCK = 64
SLOTS = 6
NBLK = 8
NLAT = 512


def band_pattern(key):
    base = jax.random.fold_in(key, 11)
    key_jitter = jax.random.fold_in(base, 1)
    key_border = jax.random.fold_in(base, 2)
    key_pick = jax.random.fold_in(base, 3)
    blocks = jnp.arange(NBLK, dtype=jnp.int32)
    distance = jnp.minimum(blocks, NBLK - 1 - blocks)
    reach_blocks = max(NBLK // 2 - 1, 1)
    jitter = jax.random.randint(key_jitter, (NBLK,), 0, 2 * K + 1, dtype=jnp.int32)
    inner = jnp.clip(3 * K - 2 * K * (distance - 1) // reach_blocks - jitter, K, 3 * K)
    border = jax.random.randint(key_border, (NBLK,), K, 2 * K + 1, dtype=jnp.int32)
    counts = jnp.where(distance == 0, border, jnp.where(distance == 1, 3 * K, inner)).astype(jnp.int32)
    pairs = jnp.arange(3 * K, dtype=jnp.int32)
    offset = pairs // K - 1
    target = blocks[:, None] + offset[None, :]
    valid = (target >= 0) & (target < NBLK)
    score = jax.random.randint(key_pick, (NBLK, 3 * K), 0, 2 ** 20, dtype=jnp.int32) * 64 + pairs[None, :]
    score = jnp.where(valid, score, score + 2 ** 27)
    order = jnp.argsort(score, axis=1).astype(jnp.int32)
    return (counts, (order // K - 1).astype(jnp.int32), (order % K).astype(jnp.int32))


def draw_band_counts(key, part):
    return band_pattern(key)[0]


def draw_band_offsets(key, part):
    return band_pattern(key)[1]


def draw_band_basis(key, part):
    return band_pattern(key)[2]


def shard_levels(stream_key, dims, cuts, least, high):
    def one(dim, blocks):
        heights = jax.random.uniform(jax.random.fold_in(jax.random.fold_in(stream_key, 6), dim), (blocks,), jnp.float32, least / len(cuts), high / len(cuts))
        return jnp.repeat(jnp.exp(heights), dims[dim] // blocks).reshape((-1,) + (1,) * (len(dims) - dim - 1))

    loudness = one(*cuts[0])
    for cut in cuts[1:]:
        loudness = loudness * one(*cut)
    return loudness


def gaussian(stream_key, extent, width, bound, shards=(), kind=jnp.bfloat16):
    entries = width * jax.random.normal(stream_key, extent, jnp.float32)
    if shards:
        entries = entries * shard_levels(stream_key, extent, shards, -0.22, 0.18)
    return jnp.clip(entries, -bound, bound).astype(kind)


def setup_inputs(seed: int = 0) -> dict:
    arg_keys = jax.random.split(jax.random.key(seed), 9)
    signal = gaussian(arg_keys[0], (NLAT, NLON, C), 1.0, 6.0, ((0, 8), (1, 4)))
    cotangent = gaussian(arg_keys[1], (NLAT, NLON, C), 1.0, 6.0, ((0, 8), (1, 4)))
    mixing = gaussian(arg_keys[2], (K, C, C), (C * K) ** -0.5, 0.25)
    coupling = gaussian(arg_keys[3], (NBLK, SLOTS, BLOCK, BLOCK), BLOCK ** -0.5, 0.75)
    filters = gaussian(arg_keys[4], (NBLK, SLOTS, 2, M), 0.7, 4.0, ((3, 4),), jnp.float32)
    band_counts = draw_band_counts(jax.random.fold_in(arg_keys[8], 71), 0)
    band_offsets = draw_band_offsets(jax.random.fold_in(arg_keys[8], 71), 0)
    band_basis = draw_band_basis(jax.random.fold_in(arg_keys[8], 71), 0)
    return dict(signal=signal, cotangent=cotangent, mixing=mixing, coupling=coupling, filters=filters, band_counts=band_counts, band_offsets=band_offsets, band_basis=band_basis)


def spectral_tables():
    longitude = jnp.arange(NLON, dtype=jnp.int32)
    wavenumber = jnp.arange(M, dtype=jnp.int32)
    product_mod = (longitude[:, None] * wavenumber[None, :]) % NLON
    phase_angle = product_mod.astype(jnp.float32) * (2.0 * math.pi / NLON)
    cosine = jnp.cos(phase_angle)
    sine_part = jnp.sin(phase_angle)
    forward = jnp.stack([cosine, -sine_part], axis=1).astype(jnp.bfloat16)
    weight = jnp.where(wavenumber == 0, 1.0, 2.0).astype(jnp.float32) / NLON
    inverse = jnp.transpose(jnp.stack([cosine, -sine_part], axis=0) * weight[None, None, :], (2, 0, 1)).astype(jnp.bfloat16)
    return forward, inverse


def apply_filter(filt, coupled, conjugate):
    real_part = filt[0][:, None, None]
    imag_part = filt[1][:, None, None]
    if conjugate:
        imag_part = -imag_part
    leading = real_part * coupled[:, 0] - imag_part * coupled[:, 1]
    trailing = real_part * coupled[:, 1] + imag_part * coupled[:, 0]
    return jnp.stack([leading, trailing], axis=1)


def reference(signal, cotangent, mixing, coupling, filters, band_counts, band_offsets, band_basis):
    forward, inverse = spectral_tables()
    forward_wide = forward.astype(jnp.float32)
    inverse_wide = inverse.astype(jnp.float32)
    mixing_wide = mixing.astype(jnp.float32)
    signal_blocks = signal.reshape(NBLK, BLOCK, NLON, C)
    cotangent_blocks = cotangent.reshape(NBLK, BLOCK, NLON, C)

    def to_modes(pieces):
        spectra = jnp.einsum('inc,npm->mpic', pieces[0].astype(jnp.float32), forward_wide).astype(jnp.bfloat16)
        gradients = jnp.einsum('inc,mpn->mpic', pieces[1].astype(jnp.float32), inverse_wide).astype(jnp.bfloat16)
        return spectra, gradients

    spectra, gradients = lax.map(to_modes, (signal_blocks, cotangent_blocks))
    border = jnp.zeros((1,) + spectra.shape[1:], jnp.bfloat16)
    spectra = jnp.concatenate([border, spectra, border], 0)
    gradients = jnp.concatenate([border, gradients, border], 0)
    zero_totals = jnp.zeros((K, M, 2, BLOCK, C), jnp.float32)

    def forward_block(block):
        def add_slot(slot, totals):
            offset = band_offsets[block, slot]
            basis = band_basis[block, slot]
            source = lax.dynamic_index_in_dim(spectra, block + offset + 1, 0, keepdims=False).astype(jnp.float32)
            coupled = jnp.einsum('rj,mpjc->mprc', coupling[block, slot].astype(jnp.float32), source)
            filtered = apply_filter(filters[block, slot], coupled, False)
            current = lax.dynamic_index_in_dim(totals, basis, 0, keepdims=False)
            return lax.dynamic_update_index_in_dim(totals, current + filtered, basis, 0)

        totals = lax.fori_loop(0, band_counts[block], add_slot, zero_totals)
        rounded = totals.astype(jnp.bfloat16).astype(jnp.float32)
        out_spectra = jnp.einsum('kmpic,kcd->mpid', rounded, mixing_wide).astype(jnp.bfloat16)
        return jnp.einsum('mpic,mpn->inc', out_spectra.astype(jnp.float32), inverse_wide).astype(jnp.bfloat16)

    def backward_block(block):
        totals = zero_totals
        for step_by in (-1, 0, 1):
            neighbour = block + step_by
            inside = (neighbour >= 0) & (neighbour < NBLK)
            safe = jnp.clip(neighbour, 0, NBLK - 1).astype(jnp.int32)
            source = lax.dynamic_index_in_dim(gradients, block + step_by + 1, 0, keepdims=False).astype(jnp.float32)
            count_there = band_counts[safe]

            def add_slot(slot, totals, safe=safe, inside=inside, source=source, count_there=count_there, step_by=step_by):
                used = inside & (slot < count_there) & (band_offsets[safe, slot] == -step_by)
                basis = band_basis[safe, slot]

                def update(totals):
                    lifted = jnp.einsum('jr,mpjc->mprc', coupling[safe, slot].astype(jnp.float32), source)
                    filtered = apply_filter(filters[safe, slot], lifted, True)
                    current = lax.dynamic_index_in_dim(totals, basis, 0, keepdims=False)
                    return lax.dynamic_update_index_in_dim(totals, current + filtered, basis, 0)

                return lax.cond(used, update, lambda kept: kept, totals)

            totals = lax.fori_loop(0, SLOTS, add_slot, totals)
        rounded = totals.astype(jnp.bfloat16).astype(jnp.float32)
        grad_spectra = jnp.einsum('kmpjd,kcd->mpjc', rounded, mixing_wide).astype(jnp.bfloat16)
        return jnp.einsum('mpjc,npm->jnc', grad_spectra.astype(jnp.float32), forward_wide).astype(jnp.bfloat16)

    block_ids = jnp.arange(NBLK, dtype=jnp.int32)
    output = lax.map(forward_block, block_ids).reshape(NLAT, NLON, C)
    signal_grad = lax.map(backward_block, block_ids).reshape(NLAT, NLON, C)
    return output, signal_grad
```

```python
import functools
import math

import jax
import jax.numpy as jnp
from jax import lax
from jax.experimental import pallas as pl
from jax.experimental.pallas import tpu as pltpu
from jax.sharding import PartitionSpec as P

K = 2


def spectral_tables(nlon, modes):
    longitude = jnp.arange(nlon, dtype=jnp.int32)
    wavenumber = jnp.arange(modes, dtype=jnp.int32)
    product_mod = longitude[:, None] * wavenumber[None, :] % nlon
    phase_angle = product_mod.astype(jnp.float32) * (2.0 * math.pi / nlon)
    wave = jnp.stack([jnp.cos(phase_angle), -jnp.sin(phase_angle)], axis=1)
    weight = jnp.where(wavenumber == 0, 1.0, 2.0).astype(jnp.float32) / nlon
    return wave.astype(jnp.bfloat16), (wave * weight).astype(jnp.bfloat16)


def modes_kernel(field_ref, wave_ref, out_ref, lanes_ref):
    parts, group, width, channels = field_ref.shape
    tall = wave_ref.shape[0]
    half = channels // 2

    def one_row(row, carry):
        column = jnp.concatenate([field_ref[a, row] for a in range(parts)], axis=0)
        spectra = jnp.dot(wave_ref[...], column, preferred_element_type=jnp.float32)
        for h in range(2):
            lanes_ref[h, pl.ds(row, tall, stride=group), :] = spectra[:, h * half : (h + 1) * half]
        return carry

    lax.fori_loop(0, group, one_row, 0)
    slab = 32

    def one_slab(i, carry):
        rows = pl.ds(pl.multiple_of(i * slab * group, slab * group), slab * group)
        for h in range(2):
            piece = lanes_ref[h, rows, :].reshape(slab, group, half)
            out_ref[pl.ds(i * slab, slab), :, h * half : (h + 1) * half] = piece.astype(out_ref.dtype)
        return carry

    lax.fori_loop(0, tall // slab, one_slab, 0)


def grid_kernel(spectra_ref, wave_ref, out_ref, lanes_ref):
    parts, group, width, channels = out_ref.shape
    tall = wave_ref.shape[1]
    half = channels // 2
    slab = 32

    def one_slab(i, carry):
        rows = pl.ds(pl.multiple_of(i * slab * group, slab * group), slab * group)
        for h in range(2):
            piece = spectra_ref[pl.ds(i * slab, slab), :, h * half : (h + 1) * half].astype(jnp.float32)
            lanes_ref[h, rows, :] = piece.reshape(slab * group, half)
        return carry

    lax.fori_loop(0, tall // slab, one_slab, 0)

    def one_row(row, carry):
        column = jnp.concatenate(
            [lanes_ref[h, pl.ds(row, tall, stride=group), :].astype(jnp.bfloat16) for h in range(2)], axis=1
        )
        field = jnp.dot(wave_ref[...], column, preferred_element_type=jnp.float32)
        for a in range(parts):
            out_ref[a, row] = field[a * width : (a + 1) * width].astype(out_ref.dtype)
        return carry

    lax.fori_loop(0, group, one_row, 0)


def transform(kernel, field, wave, shape):
    tall, group, channels = field.shape if len(field.shape) == 3 else shape
    return pl.pallas_call(
        kernel,
        out_shape=jax.ShapeDtypeStruct(shape, field.dtype),
        in_specs=[pl.BlockSpec(memory_space=pltpu.VMEM)] * 2,
        out_specs=pl.BlockSpec(memory_space=pltpu.VMEM),
        scratch_shapes=[pltpu.VMEM((2, tall * group, channels // 2), jnp.float32)],
        compiler_params=pltpu.CompilerParams(vmem_limit_bytes=40 * 2**20),
        cost_estimate=pl.CostEstimate(
            flops=2 * wave.size * group * channels, bytes_accessed=4 * field.size, transcendentals=0
        ),
    )(field, wave)


def couple_kernel(own_ref, low_ref, high_ref, weave_ref, gains_ref, mix_ref, out_ref):
    parts, step, _, group, channels = own_ref.shape
    span = 2 * parts * group

    def whole_column(ref, mode):
        if group % 16 == 0:
            return jnp.concatenate([ref[a, mode, p] for p in range(2) for a in range(parts)], axis=0)
        pieces = [ref[a, mode, p].astype(jnp.float32) for p in range(2) for a in range(parts)]
        return jnp.concatenate(pieces, axis=0).astype(jnp.bfloat16)

    def one_mode(mode, carry):
        sources = [whole_column(ref, mode) for ref in (low_ref, own_ref, high_ref)]
        source = jnp.concatenate(sources, axis=0)
        gains = gains_ref[mode]
        total = jnp.zeros((span, channels), jnp.float32)
        for k in range(K):
            matrix = jnp.concatenate(
                [(weave_ref[k] * gains[2 * k + p][None, :]).astype(jnp.bfloat16) for p in range(2)], axis=0
            )
            summed = jnp.dot(matrix, source, preferred_element_type=jnp.float32)
            total += jnp.dot(summed.astype(jnp.bfloat16), mix_ref[k], preferred_element_type=jnp.float32)
        for p in range(2):
            for a in range(parts):
                first = (p * parts + a) * group
                out_ref[a, mode, p] = total[first : first + group].astype(out_ref.dtype)
        return carry

    lax.fori_loop(0, step, one_mode, 0, unroll=4)


def couple(own, low, high, weave, gains, mix):
    parts, modes, _, group, channels = own.shape
    span = 2 * parts * group
    step = 8
    field = pl.BlockSpec((parts, step, 2, group, channels), lambda i: (0, i, 0, 0, 0))
    return pl.pallas_call(
        couple_kernel,
        grid=(modes // step,),
        out_shape=jax.ShapeDtypeStruct(own.shape, own.dtype),
        in_specs=[
            field,
            field,
            field,
            pl.BlockSpec(weave.shape, lambda i: (0, 0, 0)),
            pl.BlockSpec((step,) + gains.shape[1:], lambda i: (i, 0, 0)),
            pl.BlockSpec(mix.shape, lambda i: (0, 0, 0)),
        ],
        out_specs=field,
        compiler_params=pltpu.CompilerParams(vmem_limit_bytes=24 * 2**20),
        cost_estimate=pl.CostEstimate(
            flops=modes * 2 * channels * span * K * (3 * span + channels),
            bytes_accessed=4 * own.size * 2,
            transcendentals=0,
        ),
    )(own, low, high, weave, gains, mix)


def dense_slots(coupling, filters, counts, offsets, basis):
    slots = coupling.shape[1]
    used = jnp.arange(slots, dtype=jnp.int32)[None] < counts[:, None]
    pairs = jnp.arange(3 * K, dtype=jnp.int32)
    hot = used[:, :, None] & (((offsets + 1) * K + basis)[:, :, None] == pairs)
    mats = jnp.zeros((coupling.shape[0], 3 * K) + coupling.shape[2:], jnp.float32)
    gains = jnp.zeros((coupling.shape[0], 3 * K) + filters.shape[2:], jnp.float32)
    for s in range(slots):
        pick = hot[:, s, :, None, None]
        mats += jnp.where(pick, coupling[:, s, None].astype(jnp.float32), 0.0)
        gains += jnp.where(pick, filters[:, s, None], 0.0)
    return (
        mats.reshape((-1, 3, K) + mats.shape[2:]),
        gains.reshape((-1, 3, K) + gains.shape[2:]),
    )


def weave_of(mats, gains):
    rows = mats.shape[2]
    weave = jnp.stack([mats, mats], axis=3)
    weave = jnp.transpose(weave, (1, 2, 0, 3, 4)).reshape(K, rows, 6 * rows)
    real, imag = gains[:, :, 0], gains[:, :, 1]
    table = jnp.stack([jnp.stack([real, -imag], 0), jnp.stack([imag, real], 0)], 0)
    table = jnp.transpose(table, (4, 3, 0, 2, 1))
    modes = table.shape[0]
    table = jnp.broadcast_to(table[..., None], table.shape + (rows,))
    return weave, table.reshape(modes, 2 * K, 6 * rows)


def per_device(signal, cotangent, mixing, coupling, filters, band_counts, band_offsets, band_basis):
    parts = lax.axis_size("azimuth")
    blocks = lax.axis_size("polar")
    me = lax.axis_index("polar")
    rows, width, channels = signal.shape
    group = rows // parts
    mode_local = filters.shape[3]
    modes = mode_local * parts
    forward, inverse = spectral_tables(width * parts, modes)

    swap = functools.partial(lax.all_to_all, axis_name="azimuth", split_axis=0, concat_axis=0)

    mats, gains = dense_slots(coupling, filters, band_counts, band_offsets, band_basis)
    weave, table = weave_of(mats[me], gains[me])
    near = [jnp.clip(me + step, 0, blocks - 1) for step in (-1, 0, 1)]
    inside = [(me + step >= 0) & (me + step < blocks) for step in (-1, 0, 1)]
    back_mats = jnp.stack([jnp.swapaxes(mats[near[i], 2 - i], 1, 2) for i in range(3)])
    back_gains = jnp.stack([jnp.where(inside[i], gains[near[i], 2 - i], 0.0) for i in range(3)])
    back_gains = back_gains * jnp.array([1.0, -1.0], jnp.float32)[:, None]
    back_weave, back_table = weave_of(back_mats, back_gains)

    tall = 2 * modes

    def by_wave(wave):
        return jnp.swapaxes(wave, 1, 2).reshape(parts * width, tall)

    def to_modes(field, wave):
        spread = swap(field.reshape(parts, group, width, channels))
        spectra = transform(modes_kernel, spread, jnp.transpose(by_wave(wave)), (tall, group, channels))
        return swap(spectra.reshape(parts, mode_local, 2, group, channels))

    def halo(own):
        low = lax.ppermute(own, "polar", [(i, i + 1) for i in range(blocks - 1)])
        high = lax.ppermute(own, "polar", [(i + 1, i) for i in range(blocks - 1)])
        return low, high

    def to_grid(spectra, wave):
        spectra = swap(spectra).reshape(tall, group, channels)
        field = transform(grid_kernel, spectra, by_wave(wave), (parts, group, width, channels))
        return swap(field).reshape(rows, width, channels)

    first = to_modes(signal, forward)
    second = to_modes(cotangent, inverse)
    first_halo = halo(first)
    second_halo = halo(second)
    out_spectra = couple(first, *first_halo, weave, table, mixing)
    grad_spectra = couple(
        second, *second_halo, back_weave, back_table, jnp.swapaxes(mixing, 1, 2)
    )
    return to_grid(out_spectra, inverse), to_grid(grad_spectra, forward)


def solution(mesh):
    return jax.shard_map(
        per_device,
        mesh=mesh,
        in_specs=(
            P("polar", "azimuth", None),
            P("polar", "azimuth", None),
            P(),
            P(),
            P(None, None, None, "azimuth"),
            P(),
            P(),
            P(),
        ),
        out_specs=(P("polar", "azimuth", None), P("polar", "azimuth", None)),
        check_vma=False,
    )
```

```python
import functools
import math

import jax
import jax.numpy as jnp
from jax import lax
from jax.experimental import pallas as pl
from jax.experimental.pallas import tpu as pltpu
from jax.sharding import PartitionSpec as P

K = 2
LANES = 128


def spectral_tables(nlon, modes):
    longitude = jnp.arange(nlon, dtype=jnp.int32)
    wavenumber = jnp.arange(modes, dtype=jnp.int32)
    product_mod = longitude[:, None] * wavenumber[None, :] % nlon
    phase_angle = product_mod.astype(jnp.float32) * (2.0 * math.pi / nlon)
    wave = jnp.stack([jnp.cos(phase_angle), -jnp.sin(phase_angle)], axis=1)
    weight = jnp.where(wavenumber == 0, 1.0, 2.0).astype(jnp.float32) / nlon
    return wave.astype(jnp.bfloat16), (wave * weight).astype(jnp.bfloat16)


def pack_kernel(field_ref, pick_ref, out_ref):
    fold = field_ref.shape[0]
    parts, _, _, lanes = out_ref.shape
    wide = jnp.concatenate([field_ref[h, 0] for h in range(fold)], axis=1)
    packed = jnp.dot(wide, pick_ref[...], preferred_element_type=jnp.float32)
    for g in range(parts):
        out_ref[g, 0] = packed[:, g * lanes : (g + 1) * lanes].astype(out_ref.dtype)


def pack(field, pick, parts, fold):
    rows, width, channels = field.shape
    slim = rows // fold
    return pl.pallas_call(
        pack_kernel,
        grid=(slim,),
        out_shape=jax.ShapeDtypeStruct((parts, slim, width, LANES), field.dtype),
        in_specs=[
            pl.BlockSpec((fold, 1, width, channels), lambda i: (0, i, 0, 0)),
            pl.BlockSpec(pick.shape, lambda i: (0, 0)),
        ],
        out_specs=pl.BlockSpec((parts, 1, width, LANES), lambda i: (0, i, 0, 0)),
        compiler_params=pltpu.CompilerParams(vmem_limit_bytes=16 * 2**20),
        cost_estimate=pl.CostEstimate(
            flops=2 * field.size * parts * LANES, bytes_accessed=4 * field.size, transcendentals=0
        ),
    )(field.reshape(fold, slim, width, channels), pick)


def mix_kernel(*refs):
    mix_ref, out_ref = refs[K:]
    fold, _, _, channels = out_ref.shape
    wide = jnp.concatenate([ref[g, 0] for ref in refs[:K] for g in range(refs[0].shape[0])], axis=1)
    mixed = jnp.dot(wide, mix_ref[...], preferred_element_type=jnp.float32)
    for h in range(fold):
        out_ref[h, 0] = mixed[:, h * channels : (h + 1) * channels].astype(out_ref.dtype)


def mix_last(fields, mix, fold):
    parts, slim, width, lanes = fields[0].shape
    channels = mix.shape[1] // fold
    out = pl.pallas_call(
        mix_kernel,
        grid=(slim,),
        out_shape=jax.ShapeDtypeStruct((fold, slim, width, channels), fields[0].dtype),
        in_specs=[pl.BlockSpec((parts, 1, width, lanes), lambda i: (0, i, 0, 0))] * K
        + [pl.BlockSpec(mix.shape, lambda i: (0, 0))],
        out_specs=pl.BlockSpec((fold, 1, width, channels), lambda i: (0, i, 0, 0)),
        compiler_params=pltpu.CompilerParams(vmem_limit_bytes=16 * 2**20),
        cost_estimate=pl.CostEstimate(
            flops=2 * slim * width * mix.size, bytes_accessed=6 * fields[0].size, transcendentals=0
        ),
    )(*fields, mix)
    return out.reshape(fold * slim, width, channels)


def modes_kernel(field_ref, wave_ref, out_ref, lanes_ref):
    parts, slim, width, lanes = field_ref.shape
    tall = wave_ref.shape[0]
    half = slim // 2

    def one_pair(row, carry):
        column = jnp.concatenate(
            [
                jnp.concatenate([field_ref[a, row + h * half] for a in range(parts)], axis=0)
                for h in range(2)
            ],
            axis=1,
        )
        spectra = jnp.dot(wave_ref[...], column, preferred_element_type=jnp.float32)
        for h in range(2):
            lanes_ref[pl.ds(row + h * half, tall, stride=slim), :] = spectra[:, h * lanes : (h + 1) * lanes]
        return carry

    lax.fori_loop(0, half, one_pair, 0)
    slab = 32

    def one_slab(i, carry):
        rows = pl.ds(pl.multiple_of(i * slab * slim, slab * slim), slab * slim)
        piece = lanes_ref[rows, :].reshape(slab, slim, lanes)
        out_ref[pl.ds(i * slab, slab)] = piece.astype(out_ref.dtype)
        return carry

    lax.fori_loop(0, tall // slab, one_slab, 0)


def grid_kernel(spectra_ref, wave_ref, out_ref, lanes_ref):
    parts, slim, width, lanes = out_ref.shape
    tall = wave_ref.shape[1]
    half = slim // 2
    slab = 32

    def one_slab(i, carry):
        rows = pl.ds(pl.multiple_of(i * slab * slim, slab * slim), slab * slim)
        lanes_ref[rows, :] = spectra_ref[pl.ds(i * slab, slab)].astype(jnp.float32).reshape(slab * slim, lanes)
        return carry

    lax.fori_loop(0, tall // slab, one_slab, 0)

    def one_pair(row, carry):
        column = jnp.concatenate(
            [
                lanes_ref[pl.ds(row + h * half, tall, stride=slim), :].astype(jnp.bfloat16)
                for h in range(2)
            ],
            axis=1,
        )
        field = jnp.dot(wave_ref[...], column, preferred_element_type=jnp.float32)
        for h in range(2):
            for a in range(parts):
                piece = field[a * width : (a + 1) * width, h * lanes : (h + 1) * lanes]
                out_ref[a, row + h * half] = piece.astype(out_ref.dtype)
        return carry

    lax.fori_loop(0, half, one_pair, 0)


def transform(kernel, field, wave, shape):
    tall, slim, lanes = field.shape if len(field.shape) == 3 else shape
    return pl.pallas_call(
        kernel,
        out_shape=jax.ShapeDtypeStruct(shape, field.dtype),
        in_specs=[pl.BlockSpec(memory_space=pltpu.VMEM)] * 2,
        out_specs=pl.BlockSpec(memory_space=pltpu.VMEM),
        scratch_shapes=[pltpu.VMEM((tall * slim, lanes), jnp.float32)],
        compiler_params=pltpu.CompilerParams(vmem_limit_bytes=40 * 2**20),
        cost_estimate=pl.CostEstimate(
            flops=2 * wave.size * slim * lanes, bytes_accessed=4 * field.size, transcendentals=0
        ),
    )(field, wave)


def couple_kernel(own_ref, low_ref, high_ref, weave_ref, gains_ref, *out_refs):
    step, span, lanes = own_ref.shape
    fold, _, rows, _ = weave_ref.shape
    slim = rows // fold
    part = lanes // fold
    owner = lax.broadcasted_iota(jnp.int32, (slim, lanes), 1) // part

    def one_mode(mode, carry):
        source = jnp.concatenate([ref[mode] for ref in (low_ref, own_ref, high_ref)], axis=0)
        gains = gains_ref[mode]
        matrix = jnp.concatenate(
            [
                (weave_ref[h, k] * gains[2 * k + p][None, :]).astype(jnp.bfloat16)
                for h in range(fold)
                for k in range(K)
                for p in range(2)
            ],
            axis=0,
        )
        spread = jnp.dot(matrix, source, preferred_element_type=jnp.float32)

        def rows_from(h, k, p, to):
            first = (((h * K + k) * 2 + p) * fold + to) * slim
            return spread[first : first + slim]

        for k in range(K):
            for p in range(2):
                total = None
                for turn in range(fold):
                    term = rows_from(0, k, p, (0 - turn) % fold)
                    for h in range(1, fold):
                        term = jnp.where(owner == h, rows_from(h, k, p, (h - turn) % fold), term)
                    if turn:
                        term = pltpu.roll(term, (fold - turn) * part, 1)
                    total = term if total is None else total + term
                out_refs[k][mode, p * slim : (p + 1) * slim] = total.astype(out_refs[k].dtype)
        return carry

    lax.fori_loop(0, step, one_mode, 0, unroll=4)


def couple(own, low, high, weave, gains):
    modes, span, lanes = own.shape
    step = 16
    field = pl.BlockSpec((step, span, lanes), lambda i: (i, 0, 0))
    return pl.pallas_call(
        couple_kernel,
        grid=(modes // step,),
        out_shape=[jax.ShapeDtypeStruct(own.shape, own.dtype)] * K,
        in_specs=[
            field,
            field,
            field,
            pl.BlockSpec(weave.shape, lambda i: (0, 0, 0, 0)),
            pl.BlockSpec((step,) + gains.shape[1:], lambda i: (i, 0, 0)),
        ],
        out_specs=[field] * K,
        compiler_params=pltpu.CompilerParams(vmem_limit_bytes=24 * 2**20),
        cost_estimate=pl.CostEstimate(
            flops=2 * modes * weave.size * 2 * lanes,
            bytes_accessed=10 * own.size,
            transcendentals=0,
        ),
    )(own, low, high, weave, gains)


def dense_slots(coupling, filters, counts, offsets, basis):
    slots = coupling.shape[1]
    used = jnp.arange(slots, dtype=jnp.int32)[None] < counts[:, None]
    pairs = jnp.arange(3 * K, dtype=jnp.int32)
    hot = used[:, :, None] & (((offsets + 1) * K + basis)[:, :, None] == pairs)
    mats = jnp.zeros((coupling.shape[0], 3 * K) + coupling.shape[2:], jnp.float32)
    gains = jnp.zeros((coupling.shape[0], 3 * K) + filters.shape[2:], jnp.float32)
    for s in range(slots):
        pick = hot[:, s, :, None, None]
        mats += jnp.where(pick, coupling[:, s, None].astype(jnp.float32), 0.0)
        gains += jnp.where(pick, filters[:, s, None], 0.0)
    return (
        mats.reshape((-1, 3, K) + mats.shape[2:]),
        gains.reshape((-1, 3, K) + gains.shape[2:]),
    )


def weave_of(mats, gains, fold):
    rows = mats.shape[2]
    slim = rows // fold
    mats = mats.reshape(3, K, rows, fold, slim)
    weave = jnp.stack([mats, mats], axis=4)
    weave = jnp.transpose(weave, (3, 1, 2, 0, 4, 5)).reshape(fold, K, rows, 6 * slim)
    real, imag = gains[:, :, 0], gains[:, :, 1]
    table = jnp.stack([jnp.stack([real, -imag], 0), jnp.stack([imag, real], 0)], 0)
    table = jnp.transpose(table, (4, 3, 0, 2, 1))
    modes = table.shape[0]
    table = jnp.broadcast_to(table[..., None], table.shape + (slim,))
    return weave, table.reshape(modes, 2 * K, 6 * slim)


def per_device(signal, cotangent, mixing, coupling, filters, band_counts, band_offsets, band_basis):
    parts = lax.axis_size("azimuth")
    blocks = lax.axis_size("polar")
    me = lax.axis_index("polar")
    rows, width, channels = signal.shape
    share = channels // parts
    fold = LANES // share
    slim = rows // fold
    filters = lax.all_gather(filters, "azimuth", axis=3, tiled=True)
    modes = filters.shape[3]
    forward, inverse = spectral_tables(width * parts, modes)

    swap = functools.partial(lax.all_to_all, axis_name="azimuth", split_axis=0, concat_axis=0)

    same = jnp.eye(fold, dtype=jnp.bfloat16)
    source = jnp.arange(fold * channels, dtype=jnp.int32)
    target = jnp.arange(parts * LANES, dtype=jnp.int32)
    origin = (target % LANES // share) * channels + target // LANES * share + target % share
    pick = (source[:, None] == origin[None, :]).astype(jnp.bfloat16)

    def widen(mix):
        mix = mix.reshape(K, parts, 1, share, 1, channels) * same.reshape(1, 1, fold, 1, fold, 1)
        return mix.reshape(K * parts * LANES, fold * channels)

    mats, gains = dense_slots(coupling, filters, band_counts, band_offsets, band_basis)
    weave, table = weave_of(mats[me], gains[me], fold)
    near = [jnp.clip(me + step, 0, blocks - 1) for step in (-1, 0, 1)]
    inside = [(me + step >= 0) & (me + step < blocks) for step in (-1, 0, 1)]
    back_mats = jnp.stack([jnp.swapaxes(mats[near[i], 2 - i], 1, 2) for i in range(3)])
    back_gains = jnp.stack([jnp.where(inside[i], gains[near[i], 2 - i], 0.0) for i in range(3)])
    back_gains = back_gains * jnp.array([1.0, -1.0], jnp.float32)[:, None]
    back_weave, back_table = weave_of(back_mats, back_gains, fold)

    tall = 2 * modes

    def by_wave(wave):
        return jnp.swapaxes(wave, 1, 2).reshape(parts * width, tall)

    def to_modes(field, wave):
        spread = swap(pack(field, pick, parts, fold))
        spectra = transform(modes_kernel, spread, jnp.transpose(by_wave(wave)), (tall, slim, LANES))
        return spectra.reshape(modes, 2 * slim, LANES)

    def halo(own):
        low = lax.ppermute(own, "polar", [(i, i + 1) for i in range(blocks - 1)])
        high = lax.ppermute(own, "polar", [(i + 1, i) for i in range(blocks - 1)])
        return low, high

    def to_grid(sums, wave):
        wave = by_wave(wave)
        shape = (parts, slim, width, LANES)
        return [swap(transform(grid_kernel, one.reshape(tall, slim, LANES), wave, shape)) for one in sums]

    first = to_modes(signal, forward)
    second = to_modes(cotangent, inverse)
    first_halo = halo(first)
    second_halo = halo(second)
    sums = couple(first, *first_halo, weave, table)
    back_sums = couple(second, *second_halo, back_weave, back_table)
    output = mix_last(to_grid(sums, inverse), widen(mixing), fold)
    back = to_grid(back_sums, forward)
    return output, mix_last(back, widen(jnp.swapaxes(mixing, 1, 2)), fold)


def solution(mesh):
    return jax.shard_map(
        per_device,
        mesh=mesh,
        in_specs=(
            P("polar", "azimuth", None),
            P("polar", "azimuth", None),
            P(),
            P(),
            P(None, None, None, "azimuth"),
            P(),
            P(),
            P(),
        ),
        out_specs=(P("polar", "azimuth", None), P("polar", "azimuth", None)),
        check_vma=False,
    )
```

```python
import functools
import math

import jax
import jax.numpy as jnp
from jax import lax
from jax.experimental import pallas as pl
from jax.experimental.pallas import tpu as pltpu
from jax.sharding import PartitionSpec as P

K = 2
LANES = 128
STEP = 4


def spectral_tables(nlon, modes):
    longitude = jnp.arange(nlon, dtype=jnp.int32)
    wavenumber = jnp.arange(modes, dtype=jnp.int32)
    product_mod = longitude[:, None] * wavenumber[None, :] % nlon
    phase_angle = product_mod.astype(jnp.float32) * (2.0 * math.pi / nlon)
    wave = jnp.stack([jnp.cos(phase_angle), -jnp.sin(phase_angle)], axis=1)
    weight = jnp.where(wavenumber == 0, 1.0, 2.0).astype(jnp.float32) / nlon
    return wave.astype(jnp.bfloat16), (wave * weight).astype(jnp.bfloat16)


def pack_kernel(field_ref, pick_ref, out_ref):
    fold, step, width, channels = field_ref.shape
    parts, _, _, lanes = out_ref.shape
    wide = jnp.concatenate([field_ref[h].reshape(step * width, channels) for h in range(fold)], axis=1)
    packed = jnp.dot(wide, pick_ref[...], preferred_element_type=jnp.float32)
    for g in range(parts):
        piece = packed[:, g * lanes : (g + 1) * lanes].astype(out_ref.dtype)
        out_ref[g] = piece.reshape(step, width, lanes)


def pack(field, pick, parts, fold):
    rows, width, channels = field.shape
    slim = rows // fold
    return pl.pallas_call(
        pack_kernel,
        grid=(slim // STEP,),
        out_shape=jax.ShapeDtypeStruct((parts, slim, width, LANES), field.dtype),
        in_specs=[
            pl.BlockSpec((fold, STEP, width, channels), lambda i: (0, i, 0, 0)),
            pl.BlockSpec(pick.shape, lambda i: (0, 0)),
        ],
        out_specs=pl.BlockSpec((parts, STEP, width, LANES), lambda i: (0, i, 0, 0)),
        compiler_params=pltpu.CompilerParams(vmem_limit_bytes=32 * 2**20),
        cost_estimate=pl.CostEstimate(
            flops=2 * field.size * parts * LANES, bytes_accessed=4 * field.size, transcendentals=0
        ),
    )(field.reshape(fold, slim, width, channels), pick)


def mix_kernel(*refs):
    mix_ref, out_ref = refs[K:]
    fold, step, width, channels = out_ref.shape
    parts, _, _, lanes = refs[0].shape
    wide = jnp.concatenate(
        [ref[g].reshape(step * width, lanes) for ref in refs[:K] for g in range(parts)], axis=1
    )
    mixed = jnp.dot(wide, mix_ref[...], preferred_element_type=jnp.float32)
    for h in range(fold):
        piece = mixed[:, h * channels : (h + 1) * channels].astype(out_ref.dtype)
        out_ref[h] = piece.reshape(step, width, channels)


def mix_last(fields, mix, fold):
    parts, slim, width, lanes = fields[0].shape
    channels = mix.shape[1] // fold
    out = pl.pallas_call(
        mix_kernel,
        grid=(slim // STEP,),
        out_shape=jax.ShapeDtypeStruct((fold, slim, width, channels), fields[0].dtype),
        in_specs=[pl.BlockSpec((parts, STEP, width, lanes), lambda i: (0, i, 0, 0))] * K
        + [pl.BlockSpec(mix.shape, lambda i: (0, 0))],
        out_specs=pl.BlockSpec((fold, STEP, width, channels), lambda i: (0, i, 0, 0)),
        compiler_params=pltpu.CompilerParams(vmem_limit_bytes=32 * 2**20),
        cost_estimate=pl.CostEstimate(
            flops=2 * slim * width * mix.size, bytes_accessed=6 * fields[0].size, transcendentals=0
        ),
    )(*fields, mix)
    return out.reshape(fold * slim, width, channels)


def modes_kernel(field_ref, wave_ref, out_ref, lanes_ref):
    parts, slim, width, lanes = field_ref.shape
    tall = wave_ref.shape[0]
    half = slim // 2

    def one_pair(row, carry):
        column = jnp.concatenate(
            [
                jnp.concatenate([field_ref[a, row + h * half] for a in range(parts)], axis=0)
                for h in range(2)
            ],
            axis=1,
        )
        spectra = jnp.dot(wave_ref[...], column, preferred_element_type=jnp.float32)
        for h in range(2):
            lanes_ref[pl.ds(row + h * half, tall, stride=slim), :] = spectra[:, h * lanes : (h + 1) * lanes]
        return carry

    lax.fori_loop(0, half, one_pair, 0)
    slab = 32

    def one_slab(i, carry):
        rows = pl.ds(pl.multiple_of(i * slab * slim, slab * slim), slab * slim)
        piece = lanes_ref[rows, :].reshape(slab, slim, lanes)
        out_ref[pl.ds(i * slab, slab)] = piece.astype(out_ref.dtype)
        return carry

    lax.fori_loop(0, tall // slab, one_slab, 0)


def grid_kernel(spectra_ref, wave_ref, out_ref, lanes_ref):
    parts, slim, width, lanes = out_ref.shape
    tall = wave_ref.shape[1]
    half = slim // 2
    slab = 32

    def one_slab(i, carry):
        rows = pl.ds(pl.multiple_of(i * slab * slim, slab * slim), slab * slim)
        lanes_ref[rows, :] = spectra_ref[pl.ds(i * slab, slab)].astype(jnp.float32).reshape(slab * slim, lanes)
        return carry

    lax.fori_loop(0, tall // slab, one_slab, 0)

    def one_pair(row, carry):
        column = jnp.concatenate(
            [
                lanes_ref[pl.ds(row + h * half, tall, stride=slim), :].astype(jnp.bfloat16)
                for h in range(2)
            ],
            axis=1,
        )
        field = jnp.dot(wave_ref[...], column, preferred_element_type=jnp.float32)
        for h in range(2):
            for a in range(parts):
                piece = field[a * width : (a + 1) * width, h * lanes : (h + 1) * lanes]
                out_ref[a, row + h * half] = piece.astype(out_ref.dtype)
        return carry

    lax.fori_loop(0, half, one_pair, 0)


def transform(kernel, field, wave, shape):
    tall, slim, lanes = field.shape if len(field.shape) == 3 else shape
    return pl.pallas_call(
        kernel,
        out_shape=jax.ShapeDtypeStruct(shape, field.dtype),
        in_specs=[pl.BlockSpec(memory_space=pltpu.VMEM)] * 2,
        out_specs=pl.BlockSpec(memory_space=pltpu.VMEM),
        scratch_shapes=[pltpu.VMEM((tall * slim, lanes), jnp.float32)],
        compiler_params=pltpu.CompilerParams(vmem_limit_bytes=40 * 2**20),
        cost_estimate=pl.CostEstimate(
            flops=2 * wave.size * slim * lanes, bytes_accessed=4 * field.size, transcendentals=0
        ),
    )(field, wave)


def couple_kernel(own_ref, low_ref, high_ref, weave_ref, gains_ref, *out_refs):
    step, span, lanes = own_ref.shape
    fold, _, rows, _ = weave_ref.shape
    slim = rows // fold
    part = lanes // fold
    owner = lax.broadcasted_iota(jnp.int32, (slim, lanes), 1) // part

    def one_mode(mode, carry):
        source = jnp.concatenate([ref[mode] for ref in (low_ref, own_ref, high_ref)], axis=0)
        gains = gains_ref[mode]
        matrix = jnp.concatenate(
            [
                (weave_ref[h, k] * gains[2 * k + p][None, :]).astype(jnp.bfloat16)
                for h in range(fold)
                for k in range(K)
                for p in range(2)
            ],
            axis=0,
        )
        spread = jnp.dot(matrix, source, preferred_element_type=jnp.float32)

        def rows_from(h, k, p, to):
            first = (((h * K + k) * 2 + p) * fold + to) * slim
            return spread[first : first + slim]

        for k in range(K):
            for p in range(2):
                total = None
                for turn in range(fold):
                    term = rows_from(0, k, p, (0 - turn) % fold)
                    for h in range(1, fold):
                        term = jnp.where(owner == h, rows_from(h, k, p, (h - turn) % fold), term)
                    if turn:
                        term = pltpu.roll(term, (fold - turn) * part, 1)
                    total = term if total is None else total + term
                out_refs[k][mode, p * slim : (p + 1) * slim] = total.astype(out_refs[k].dtype)
        return carry

    lax.fori_loop(0, step, one_mode, 0, unroll=4)


def couple(own, low, high, weave, gains):
    modes, span, lanes = own.shape
    step = 16
    field = pl.BlockSpec((step, span, lanes), lambda i: (i, 0, 0))
    return pl.pallas_call(
        couple_kernel,
        grid=(modes // step,),
        out_shape=[jax.ShapeDtypeStruct(own.shape, own.dtype)] * K,
        in_specs=[
            field,
            field,
            field,
            pl.BlockSpec(weave.shape, lambda i: (0, 0, 0, 0)),
            pl.BlockSpec((step,) + gains.shape[1:], lambda i: (i, 0, 0)),
        ],
        out_specs=[field] * K,
        compiler_params=pltpu.CompilerParams(vmem_limit_bytes=24 * 2**20),
        cost_estimate=pl.CostEstimate(
            flops=2 * modes * weave.size * 2 * lanes,
            bytes_accessed=10 * own.size,
            transcendentals=0,
        ),
    )(own, low, high, weave, gains)


def dense_slots(coupling, filters, counts, offsets, basis):
    slots = coupling.shape[1]
    used = jnp.arange(slots, dtype=jnp.int32)[None] < counts[:, None]
    pairs = jnp.arange(3 * K, dtype=jnp.int32)
    hot = used[:, :, None] & (((offsets + 1) * K + basis)[:, :, None] == pairs)
    mats = jnp.zeros((coupling.shape[0], 3 * K) + coupling.shape[2:], jnp.float32)
    gains = jnp.zeros((coupling.shape[0], 3 * K) + filters.shape[2:], jnp.float32)
    for s in range(slots):
        pick = hot[:, s, :, None, None]
        mats += jnp.where(pick, coupling[:, s, None].astype(jnp.float32), 0.0)
        gains += jnp.where(pick, filters[:, s, None], 0.0)
    return (
        mats.reshape((-1, 3, K) + mats.shape[2:]),
        gains.reshape((-1, 3, K) + gains.shape[2:]),
    )


def weave_of(mats, gains, fold):
    rows = mats.shape[2]
    slim = rows // fold
    mats = mats.reshape(3, K, rows, fold, slim)
    weave = jnp.stack([mats, mats], axis=4)
    weave = jnp.transpose(weave, (3, 1, 2, 0, 4, 5)).reshape(fold, K, rows, 6 * slim)
    real, imag = gains[:, :, 0], gains[:, :, 1]
    table = jnp.stack([jnp.stack([real, -imag], 0), jnp.stack([imag, real], 0)], 0)
    table = jnp.transpose(table, (4, 3, 0, 2, 1))
    modes = table.shape[0]
    table = jnp.broadcast_to(table[..., None], table.shape + (slim,))
    return weave, table.reshape(modes, 2 * K, 6 * slim)


def per_device(signal, cotangent, mixing, coupling, filters, band_counts, band_offsets, band_basis):
    parts = lax.axis_size("azimuth")
    blocks = lax.axis_size("polar")
    me = lax.axis_index("polar")
    rows, width, channels = signal.shape
    share = channels // parts
    fold = LANES // share
    slim = rows // fold
    filters = lax.all_gather(filters, "azimuth", axis=3, tiled=True)
    filters, signal = lax.optimization_barrier((filters, signal))
    modes = filters.shape[3]
    forward, inverse = spectral_tables(width * parts, modes)

    swap = functools.partial(lax.all_to_all, axis_name="azimuth", split_axis=0, concat_axis=0)

    same = jnp.eye(fold, dtype=jnp.bfloat16)
    source = jnp.arange(fold * channels, dtype=jnp.int32)
    target = jnp.arange(parts * LANES, dtype=jnp.int32)
    origin = (target % LANES // share) * channels + target // LANES * share + target % share
    pick = (source[:, None] == origin[None, :]).astype(jnp.bfloat16)

    def widen(mix):
        mix = mix.reshape(K, parts, 1, share, 1, channels) * same.reshape(1, 1, fold, 1, fold, 1)
        return mix.reshape(K * parts * LANES, fold * channels)

    mats, gains = dense_slots(coupling, filters, band_counts, band_offsets, band_basis)
    weave, table = weave_of(mats[me], gains[me], fold)
    near = [jnp.clip(me + step, 0, blocks - 1) for step in (-1, 0, 1)]
    inside = [(me + step >= 0) & (me + step < blocks) for step in (-1, 0, 1)]
    back_mats = jnp.stack([jnp.swapaxes(mats[near[i], 2 - i], 1, 2) for i in range(3)])
    back_gains = jnp.stack([jnp.where(inside[i], gains[near[i], 2 - i], 0.0) for i in range(3)])
    back_gains = back_gains * jnp.array([1.0, -1.0], jnp.float32)[:, None]
    back_weave, back_table = weave_of(back_mats, back_gains, fold)

    tall = 2 * modes

    def by_wave(wave):
        return jnp.swapaxes(wave, 1, 2).reshape(parts * width, tall)

    def to_modes(spread, wave):
        spectra = transform(modes_kernel, spread, jnp.transpose(by_wave(wave)), (tall, slim, LANES))
        return spectra.reshape(modes, 2 * slim, LANES)

    def halo(own):
        low = lax.ppermute(own, "polar", [(i, i + 1) for i in range(blocks - 1)])
        high = lax.ppermute(own, "polar", [(i + 1, i) for i in range(blocks - 1)])
        return low, high

    def to_grid(sums, wave):
        wave = by_wave(wave)
        shape = (parts, slim, width, LANES)
        return [swap(transform(grid_kernel, one.reshape(tall, slim, LANES), wave, shape)) for one in sums]

    first = swap(pack(signal, pick, parts, fold))
    first, second = lax.optimization_barrier((first, pack(cotangent, pick, parts, fold)))
    first = to_modes(first, forward)
    first_halo = halo(first)
    second = to_modes(swap(second), inverse)
    first, second = lax.optimization_barrier((first, second))
    second_halo = halo(second)
    sums = couple(first, *first_halo, weave, table)
    back_sums = couple(second, *second_halo, back_weave, back_table)
    output = mix_last(to_grid(sums, inverse), widen(mixing), fold)
    back = to_grid(back_sums, forward)
    return output, mix_last(back, widen(jnp.swapaxes(mixing, 1, 2)), fold)


def solution(mesh):
    return jax.shard_map(
        per_device,
        mesh=mesh,
        in_specs=(
            P("polar", "azimuth", None),
            P("polar", "azimuth", None),
            P(),
            P(),
            P(None, None, None, "azimuth"),
            P(),
            P(),
            P(),
        ),
        out_specs=(P("polar", "azimuth", None), P("polar", "azimuth", None)),
        check_vma=False,
    )
```
